32 devices in a mesh: groups: 2 (over x), dp: 16 (over z, y, core).
Axes of the slice: x: 2, y: 2, z: 4, core: 2. Of those that a mesh axis runs over, the one named last changes fastest.
Arguments:
- hidden_in: bfloat16 [32768, 768], P(('groups', 'dp')), parts along dimension 0, may hold values from -6 to 6
- up_weight: bfloat16 [768, 3072], replicated, may hold values from -0.21875 to 0.21875
- up_bias: float32 [3072], replicated, may hold values from -3 to 3
- down_weight: bfloat16 [3072, 768], replicated, may hold values from -0.109375 to 0.109375
- down_bias: float32 [768], replicated, may hold values from -3 to 3
- norm_gain: float32 [768], replicated, may hold values from 0.1 to 1.9
- norm_shift: float32 [768], replicated, may hold values from -3 to 3
- proj_weight: bfloat16 [768, 128], replicated, may hold values from -0.21875 to 0.21875
- centroids: bfloat16 [65536, 128], P('dp'), may hold values from -0.5 to 0.5
- lengths: int32 [256], P(('groups', 'dp')), parts along dimension 0, may hold values from 1 to 128, 12288 in all
- owners: int32 [32768, 1], P(('groups', 'dp')), parts along dimension 0, may hold values from 0 to 15; in each aligned block of 1024 rows (0 to 1023, 1024 to 2047, ...) at most 128 rows name the same one
- local_ids: int32 [32768], P(('groups', 'dp')), parts along dimension 0, may hold values from 0 to 4095
Outputs:
- residuals: bfloat16 [32768, 128], P(('groups', 'dp')), parts along dimension 0
The draws below stay inside these ranges and needn't reach their ends.
There are 2 independent parts, one for each index of `groups`. The reference program is written for one: setup_inputs(seed, part) draws one part's arguments, and reference() takes and returns one part's arrays. A program takes and returns all parts, laid end to end along the dimension named above; an argument that names none is the same for every part. Nothing has to cross between parts.
Inputs may be any that keep to these rules, and one draw needn't show every extreme that they name: `owners`: in the rows of one device (1024 rows) no owner is named by more than 128 rows, and one owner by exactly 128; every owner is named somewhere. All lengths together sum to 12288.
All inputs are finite; a program needn't handle non-finite values. No bound on the sum of `lengths` on one device may be relied on, other than what follows from the above.
Results may differ from the reference program's by a relative error of at most 0.0051.
Values may be sent and summed in bfloat16 or wider, within the bound.
No kernel may reach another device: no remote copies, remote signals or barrier semaphores. Data moves between devices by JAX's collectives and lax.ppermute only.
A program may use at most 64 MiB of HBM per device.

```python
import math
import jax
import jax.numpy as jnp
import numpy as np
from jax import lax

D = 768
FF = 3072
OUT = 128
LEN = 128
TOK_DEV = 1024
CENT_DEV = 4096
TOKENS = 16384
PASSAGES = 128
CENTROIDS = 65536
CAP = 128
N_DP = 16


def set_ends(array, stream_key, least, largest):
    index_at = [jax.random.randint(jax.random.fold_in(stream_key, axis), (), 0, length) for axis, length in enumerate(array.shape)]
    longest = array.shape.index(max(array.shape))
    beside = index_at[:longest] + [(index_at[longest] + 1) % array.shape[longest]] + index_at[longest + 1:]
    return array.at[tuple(index_at)].set(least).at[tuple(beside)].set(largest)


def steps_of(stream_key, extent, cuts, smallest, largest):
    gain, own = 1.0, jax.random.fold_in(stream_key, 6)
    for dim, parts in cuts:
        steps = jnp.exp(jax.random.uniform(jax.random.fold_in(own, dim), (parts,), jnp.float32, smallest / len(cuts), largest / len(cuts)))
        gain = gain * jnp.repeat(steps, extent[dim] // parts).reshape([-1 if axis == dim else 1 for axis in range(len(extent))])
    return gain


def profile(count, total, most, skew):
    portions = [(1 << 20) // math.isqrt(standing ** skew) + 1 for standing in range(2, count + 1)]
    rest, counts = total - most - (count - 1), [1] * (count - 1)
    while rest > 0:
        candidates = [i for i in range(count - 1) if counts[i] < most]
        mass, remaining = sum([portions[i] for i in candidates]), rest
        for i in candidates:
            extra = min(most - counts[i], max(1, remaining * portions[i] // mass), rest)
            counts[i] = counts[i] + extra
            rest = rest - extra
    return np.array([most] + counts)


def uneven(own_key, amount, total, limit, slope):
    if amount == 2:
        one = jax.random.randint(own_key, (), max(1, total - limit), min(limit, total - 1) + 1)
        return jnp.stack([one, total - one])
    sizes = jnp.asarray(profile(amount, total, limit, slope), jnp.int32)
    couples = (amount - 1) // 2
    source_of, taker = sizes[1:1 + 2 * couples:2], sizes[2:2 + 2 * couples:2]
    room = jnp.minimum(source_of - 1, limit - taker)
    shifted = jax.random.randint(jax.random.fold_in(own_key, 1), (couples,), 0, 1 << 20) % (room + 1)
    sizes = sizes.at[1:1 + 2 * couples:2].set(source_of - shifted).at[2:2 + 2 * couples:2].set(taker + shifted)
    return sizes[jax.random.permutation(jax.random.fold_in(own_key, 2), amount)]


def assign_block(stream_key, own, number, rows, number_of, top, bound, lean):
    sequence = jax.random.permutation(stream_key, number_of)
    heavy_load, usual = load_shares(number_of, rows * top, bound, lean, True), load_shares(number_of, rows * top, bound, lean, False)
    places = jnp.arange(number_of)

    def named(sizes, offset_by):
        used = int((sizes > 0).sum())
        fixed = max(1, used // 4)
        shifted = fixed + (places - fixed + offset_by * (used - fixed)) % max(1, number_of - fixed)
        return jnp.zeros((number_of,), jnp.int32).at[sequence[jnp.where(places < fixed, places, shifted)]].set(jnp.asarray(sizes, jnp.int32))

    sizes = jnp.where(number % 4 == 0, named(heavy_load, number // 4), named(usual, number - number // 4 - 1))
    mixed = jax.random.permutation(jax.random.fold_in(own, 3), number_of)
    donor, receiver = mixed[0:number_of // 2 * 2:2], mixed[1:number_of // 2 * 2:2]
    room = jnp.minimum(sizes[donor] - 1, bound - sizes[receiver]) // 2
    room = jnp.where((donor == sequence[0]) | (receiver == sequence[0]) | (sizes[receiver] == 0), 0, jnp.maximum(room, 0))
    shifted = jax.random.randint(jax.random.fold_in(own, 4), (number_of // 2,), 0, 1 << 20) % (room + 1)
    sizes = sizes.at[donor].add(-shifted).at[receiver].add(shifted)
    items = jnp.searchsorted(jnp.cumsum(sizes), jnp.arange(rows * top), side="right").astype(jnp.int32)
    table = items.reshape(top, rows).T
    table = table[jax.random.permutation(jax.random.fold_in(own, 1), rows)]
    offset_by = jax.random.randint(jax.random.fold_in(own, 2), (rows, 1), 0, top)
    return jnp.take_along_axis(table, (jnp.arange(top)[None, :] + offset_by) % top, axis=1)


def load_shares(count, total, bound, slope, full):
    weights = [(1 << 20) // math.isqrt(rank ** slope) + 1 for rank in range(1, count + 1)]
    largest = bound if full else min(bound, max(-(-total // count), total * weights[0] // sum(weights)))
    least = 1 if total - largest >= count - 1 else 0
    counts, rest = [largest] + [least] * (count - 1), total - largest - least * (count - 1)
    while rest > 0:
        free = [i for i in range(1, count) if counts[i] < largest] or [i for i in range(1, count) if counts[i] < bound]
        whole, left = sum([weights[i] for i in free]), rest
        for i in free:
            extra = min(bound - counts[i], max(1, left * weights[i] // whole), rest)
            counts[i] = counts[i] + extra
            rest = rest - extra
    return np.array(counts)


def scatter_about(own_key, dims, scale, most, shards=(), kind=jnp.bfloat16):
    gain = steps_of(own_key, dims, shards, -0.22, 0.18) if shards else 1.0
    drawn = jax.random.normal(own_key, dims, jnp.float32) * scale * gain
    return jnp.minimum(jnp.maximum(drawn, -most), most).astype(kind)


def setup_inputs(seed: int = 0, part: int = 0) -> dict:
    arg_keys = jax.random.split(jax.random.key(seed), 13)
    own_keys = jax.random.split(jax.random.fold_in(arg_keys[12], part), 13)
    hidden_in = scatter_about(own_keys[0], (TOKENS, D), 1.0, 6.0, ((0, 16),))
    up_weight = scatter_about(arg_keys[1], (D, FF), D ** -0.5, 0.21875)
    up_bias = scatter_about(arg_keys[2], (FF,), 0.5, 3.0, (), jnp.float32)
    down_weight = scatter_about(arg_keys[3], (FF, D), FF ** -0.5, 0.109375)
    down_bias = scatter_about(arg_keys[4], (D,), 0.5, 3.0, (), jnp.float32)
    norm_gain = jnp.clip(1.0 + 0.18 * jax.random.normal(arg_keys[5], (D,), jnp.float32), 0.1, 1.9)
    norm_shift = scatter_about(arg_keys[6], (D,), 0.5, 3.0, (), jnp.float32)
    proj_weight = scatter_about(arg_keys[7], (D, OUT), D ** -0.5, 0.21875)
    centroids = scatter_about(arg_keys[8], (CENTROIDS, OUT), OUT ** -0.5, 0.5, ((0, 16),))
    lengths = uneven(own_keys[9], PASSAGES, PASSAGES * LEN * 3 // 4, LEN, 2).astype(jnp.int32)
    owners_keys = jax.random.split(jax.random.fold_in(own_keys[10], 1), TOKENS // TOK_DEV)
    owners_turns = jax.random.permutation(jax.random.fold_in(own_keys[10], 3), TOKENS // TOK_DEV)
    owners = jax.vmap(lambda own, number: assign_block(jax.random.fold_in(own_keys[10], 2), own, number, TOK_DEV, N_DP, 1, CAP, 2))(owners_keys, owners_turns).reshape((TOKENS, 1))
    local_ids = set_ends(jax.random.randint(own_keys[11], (TOKENS,), 0, CENT_DEV), jax.random.fold_in(own_keys[11], 1), 0, CENT_DEV - 1).astype(jnp.int32)
    return dict(hidden_in=hidden_in, up_weight=up_weight, up_bias=up_bias, down_weight=down_weight, down_bias=down_bias, norm_gain=norm_gain, norm_shift=norm_shift, proj_weight=proj_weight, centroids=centroids, lengths=lengths, owners=owners, local_ids=local_ids)


def encode_block(block, up_weight, up_bias, down_weight, down_bias, norm_gain, norm_shift, proj_weight):
    up_proj = jnp.dot(block, up_weight, preferred_element_type=jnp.float32) + up_bias
    activated = jax.nn.gelu(up_proj, approximate=False).astype(jnp.bfloat16)
    ffn_out = jnp.dot(activated, down_weight, preferred_element_type=jnp.float32) + down_bias + block.astype(jnp.float32)
    center = lax.optimization_barrier(jnp.mean(ffn_out, axis=1, keepdims=True))
    spread = lax.optimization_barrier(jnp.mean((ffn_out - center) ** 2, axis=1, keepdims=True))
    normed = ((ffn_out - center) / jnp.sqrt(spread + 1e-05) * norm_gain + norm_shift).astype(jnp.bfloat16)
    projected = jnp.dot(normed, proj_weight, preferred_element_type=jnp.float32)
    scale = jnp.sqrt(lax.optimization_barrier(jnp.sum(projected * projected, axis=1, keepdims=True)) + 1e-06)
    return (projected / scale).astype(jnp.bfloat16)

def reference(hidden_in, up_weight, up_bias, down_weight, down_bias, norm_gain, norm_shift, proj_weight, centroids, lengths, owners, local_ids):
    blocks = hidden_in.reshape(-1, TOK_DEV, D)
    embedded = lax.map(lambda block: encode_block(block, up_weight, up_bias, down_weight, down_bias, norm_gain, norm_shift, proj_weight), blocks)
    embedded = embedded.reshape(-1, OUT)
    center_index = (owners[:, 0] * CENT_DEV + local_ids).astype(jnp.int32)
    centers = centroids[center_index]
    difference = embedded.astype(jnp.float32) - centers.astype(jnp.float32)
    scale = jnp.sqrt(lax.optimization_barrier(jnp.sum(difference * difference, axis=1, keepdims=True)) + 1e-06)
    slots = jnp.arange(TOKENS, dtype=jnp.int32)
    position = slots % LEN
    passage_len = lengths[(slots // LEN).astype(jnp.int32)]
    alive = (position < passage_len)[:, None]
    return jnp.where(alive, difference / scale, 0.0).astype(jnp.bfloat16)
```

```python
import functools

import jax
import jax.numpy as jnp
from jax import lax
from jax.experimental import pallas as pl
from jax.experimental.pallas import tpu as pltpu
from jax.sharding import PartitionSpec as P

LEN = 128
LANES = 128
LOW = 64
VMEM_BYTES = 48 * 2**20
VMEM = pl.BlockSpec(memory_space=pltpu.VMEM)
SMEM = pl.BlockSpec(memory_space=pltpu.SMEM)
HBM = pl.BlockSpec(memory_space=pl.ANY)


def plan_kernel(owners_ref, ids_ref, slots_ref, asked_ref):
    n_owners, capacity = asked_ref.shape
    n_rows = owners_ref.shape[0]
    owner_iota = lax.broadcasted_iota(jnp.int32, (n_owners, LANES), 0)
    slot_iota = lax.broadcasted_iota(jnp.int32, (capacity, LANES), 0)
    before = lax.broadcasted_iota(jnp.int32, (LANES, LANES), 0) < lax.broadcasted_iota(
        jnp.int32, (LANES, LANES), 1
    )
    counter = jnp.concatenate(
        [before.astype(jnp.float32), jnp.ones((LANES, LANES), jnp.float32)], axis=1
    ).astype(jnp.bfloat16)
    named = jnp.zeros((n_owners, LANES), jnp.float32)
    high = jnp.zeros((n_owners, capacity), jnp.float32)
    low = jnp.zeros((n_owners, capacity), jnp.float32)
    for row in range(n_rows):
        owner_row = owners_ref[row : row + 1, :]
        ids_row = ids_ref[row : row + 1, :]
        hot = (owner_iota == owner_row).astype(jnp.float32)
        counts = jnp.dot(hot.astype(jnp.bfloat16), counter, preferred_element_type=jnp.float32)
        slot = jnp.sum(hot * (counts[:, :LANES] + named), axis=0, keepdims=True).astype(jnp.int32)
        named = named + counts[:, LANES:]
        slots_ref[row : row + 1, :] = owner_row * capacity + slot
        placed = (slot_iota == slot).astype(jnp.float32).astype(jnp.bfloat16)
        parts = jnp.concatenate(
            [
                hot * (ids_row // LOW).astype(jnp.float32),
                hot * (ids_row % LOW).astype(jnp.float32),
            ],
            axis=0,
        ).astype(jnp.bfloat16)
        both = lax.dot_general(
            parts, placed, (((1,), (1,)), ((), ())), preferred_element_type=jnp.float32
        )
        high = high + both[:n_owners]
        low = low + both[n_owners:]
    asked_ref[...] = high.astype(jnp.int32) * LOW + low.astype(jnp.int32)


def plan(owners, local_ids, n_owners, capacity):
    rows = owners.shape[0]
    return pl.pallas_call(
        plan_kernel,
        in_specs=[VMEM, VMEM],
        out_specs=[VMEM, VMEM],
        out_shape=[
            jax.ShapeDtypeStruct((rows, LANES), jnp.int32),
            jax.ShapeDtypeStruct((n_owners, capacity), jnp.int32),
        ],
        name="plan",
    )(owners, local_ids)


def gather_kernel(asked_ref, table_ref, out_ref, table_f32, out_f32):
    n_owners, capacity = asked_ref.shape
    table_f32[...] = table_ref[...].astype(jnp.float32)

    def step(owner, carry):
        for slot in range(capacity):
            row = asked_ref[owner, slot]
            out_f32[pl.ds(owner * capacity + slot, 1), :] = table_f32[pl.ds(row, 1), :]
        return carry

    lax.fori_loop(0, n_owners, step, 0)
    out_ref[...] = out_f32[...].astype(jnp.bfloat16)


def gather_rows(asked, table):
    rows = asked.shape[0] * asked.shape[1]
    width = table.shape[1]
    return pl.pallas_call(
        gather_kernel,
        in_specs=[SMEM, VMEM],
        out_specs=VMEM,
        out_shape=jax.ShapeDtypeStruct((rows, width), jnp.bfloat16),
        scratch_shapes=[
            pltpu.VMEM(table.shape, jnp.float32),
            pltpu.VMEM((rows, width), jnp.float32),
        ],
        compiler_params=pltpu.CompilerParams(vmem_limit_bytes=VMEM_BYTES),
        name="gather_rows",
    )(asked, table)


def finish_kernel(slots_ref, lengths_ref, first_ref, second_ref, centers_ref, out_ref, centers_f32, mine):
    centers_f32[...] = centers_ref[...].astype(jnp.float32)
    n_passages = out_ref.shape[0] // LEN
    split = first_ref.shape[0] // LEN

    def step(passage, carry):
        for position in range(LEN):
            row = slots_ref[passage, position]
            mine[pl.ds(passage * LEN + position, 1), :] = centers_f32[pl.ds(row, 1), :]
        return carry

    lax.fori_loop(0, n_passages, step, 0)
    position = lax.broadcasted_iota(jnp.int32, (LEN, 1), 0)
    for passage in range(n_passages):
        at = slice(passage * LEN, (passage + 1) * LEN)
        if passage < split:
            embedded = first_ref[at, :]
        else:
            embedded = second_ref[(passage - split) * LEN : (passage - split + 1) * LEN, :]
        difference = embedded.astype(jnp.float32) - mine[at, :]
        total = jnp.sum(difference * difference, axis=1, keepdims=True)
        result = difference * lax.rsqrt(total + 1e-06)
        alive = position < lengths_ref[passage]
        out_ref[at, :] = jnp.where(alive, result, 0.0).astype(jnp.bfloat16)


def finish(slots, lengths, first, second, centers):
    rows = slots.shape[0] * slots.shape[1]
    width = centers.shape[1]
    return pl.pallas_call(
        finish_kernel,
        in_specs=[SMEM, SMEM, VMEM, VMEM, VMEM],
        out_specs=VMEM,
        out_shape=jax.ShapeDtypeStruct((rows, width), jnp.bfloat16),
        scratch_shapes=[
            pltpu.VMEM(centers.shape, jnp.float32),
            pltpu.VMEM((rows, width), jnp.float32),
        ],
        compiler_params=pltpu.CompilerParams(vmem_limit_bytes=VMEM_BYTES),
        name="finish",
    )(slots, lengths, first, second, centers)


def encode_kernel(
    chunk, rows_ref, up_hbm, up_bias_ref, down_hbm, down_bias_ref, gain_ref, shift_ref, proj_ref,
    out_ref, up_vmem, down_vmem, arrived,
):
    n_chunks = up_vmem.shape[0]

    def up_copy(index):
        return pltpu.make_async_copy(
            up_hbm.at[:, pl.ds(index * chunk, chunk)], up_vmem.at[index], arrived.at[0, index]
        )

    def down_copy(index):
        return pltpu.make_async_copy(
            down_hbm.at[pl.ds(index * chunk, chunk), :], down_vmem.at[index], arrived.at[1, index]
        )

    def tile(first):
        rows = rows_ref[...]
        total = None
        for index in range(n_chunks):
            if first:
                up_copy(index).wait()
            up_proj = (
                jnp.dot(rows, up_vmem[index], preferred_element_type=jnp.float32)
                + up_bias_ref[:, index * chunk : (index + 1) * chunk]
            )
            activated = (0.5 * up_proj * (1.0 + lax.erf(up_proj * 0.7071067811865476))).astype(
                jnp.bfloat16
            )
            if first:
                down_copy(index).wait()
            part = jnp.dot(activated, down_vmem[index], preferred_element_type=jnp.float32)
            total = part if total is None else total + part
        ffn_out = total + down_bias_ref[...] + rows.astype(jnp.float32)
        center = jnp.mean(ffn_out, axis=1, keepdims=True)
        centered = ffn_out - center
        spread = jnp.mean(centered * centered, axis=1, keepdims=True)
        normed = (centered * lax.rsqrt(spread + 1e-05) * gain_ref[...] + shift_ref[...]).astype(
            jnp.bfloat16
        )
        projected = jnp.dot(normed, proj_ref[...], preferred_element_type=jnp.float32)
        size = jnp.sum(projected * projected, axis=1, keepdims=True)
        out_ref[...] = (projected * lax.rsqrt(size + 1e-06)).astype(jnp.bfloat16)

    @pl.when(pl.program_id(0) == 0)
    def _():
        for index in range(n_chunks):
            up_copy(index).start()
            down_copy(index).start()
        tile(True)

    @pl.when(pl.program_id(0) > 0)
    def _():
        tile(False)


def encode(hidden_in, weights, start, rows, tile_rows=256, chunk=768):
    up_weight, up_bias, down_weight, down_bias, norm_gain, norm_shift, proj_weight = weights
    width, hidden = up_weight.shape
    out_width = proj_weight.shape[1]
    n_chunks = hidden // chunk
    start_tile = start // tile_rows

    def whole(array):
        return pl.BlockSpec(array.shape, lambda index: (0, 0))

    return pl.pallas_call(
        functools.partial(encode_kernel, chunk),
        grid=(rows // tile_rows,),
        in_specs=[
            pl.BlockSpec((tile_rows, width), lambda index: (index + start_tile, 0)),
            HBM,
            whole(up_bias),
            HBM,
            whole(down_bias),
            whole(norm_gain),
            whole(norm_shift),
            whole(proj_weight),
        ],
        out_specs=pl.BlockSpec((tile_rows, out_width), lambda index: (index, 0)),
        out_shape=jax.ShapeDtypeStruct((rows, out_width), jnp.bfloat16),
        scratch_shapes=[
            pltpu.VMEM((n_chunks, width, chunk), jnp.bfloat16),
            pltpu.VMEM((n_chunks, chunk, width), jnp.bfloat16),
            pltpu.SemaphoreType.DMA((2, n_chunks)),
        ],
        compiler_params=pltpu.CompilerParams(vmem_limit_bytes=VMEM_BYTES),
        cost_estimate=pl.CostEstimate(
            flops=2 * rows * (2 * width * hidden + width * out_width),
            bytes_accessed=4 * width * hidden + 2 * rows * width,
            transcendentals=0,
        ),
        name="encode",
    )(hidden_in, up_weight, up_bias, down_weight, down_bias, norm_gain, norm_shift, proj_weight)


def body(
    hidden_in, up_weight, up_bias, down_weight, down_bias, norm_gain, norm_shift, proj_weight,
    centroids, lengths, owners, local_ids,
):
    n_devices = lax.axis_size("dp")
    token_rows = hidden_in.shape[0]
    width_out = proj_weight.shape[1]
    capacity = max(2, 2 * token_rows // n_devices)
    weights = (
        up_weight, up_bias[None, :], down_weight, down_bias[None, :],
        norm_gain[None, :], norm_shift[None, :], proj_weight,
    )
    early = token_rows // 4
    slots, asked = plan(
        owners.reshape(-1, LANES), local_ids.reshape(-1, LANES), n_devices, capacity
    )
    arrived = lax.all_to_all(asked, "dp", split_axis=0, concat_axis=0, tiled=True)
    first = encode(hidden_in, weights, 0, early)
    arrived, first = lax.optimization_barrier((arrived, first))
    rows = gather_rows(arrived, centroids)
    hidden_late, rows = lax.optimization_barrier((hidden_in, rows))
    centers = lax.all_to_all(
        rows.reshape(n_devices, capacity, width_out), "dp", split_axis=0, concat_axis=0, tiled=True
    )
    second = encode(hidden_late, weights, early, token_rows - early)
    centers, second = lax.optimization_barrier((centers, second))
    return finish(slots, lengths, first, second, centers.reshape(-1, width_out))


def solution(mesh):
    in_specs = (
        P(("groups", "dp"), None),
        P(),
        P(),
        P(),
        P(),
        P(),
        P(),
        P(),
        P("dp", None),
        P(("groups", "dp")),
        P(("groups", "dp"), None),
        P(("groups", "dp")),
    )
    out_specs = P(("groups", "dp"), None)
    return jax.shard_map(body, mesh=mesh, in_specs=in_specs, out_specs=out_specs, check_vma=False)
```

```python
import functools

import jax
import jax.numpy as jnp
from jax import lax
from jax.experimental import pallas as pl
from jax.experimental.pallas import tpu as pltpu
from jax.sharding import PartitionSpec as P

LEN = 128
LANES = 128
LOW = 64
COUNT = 65536
GROUP = 16
AHEAD = 2
VMEM_BYTES = 60 * 2**20
VMEM = pl.BlockSpec(memory_space=pltpu.VMEM)
SMEM = pl.BlockSpec(memory_space=pltpu.SMEM)
HBM = pl.BlockSpec(memory_space=pltpu.HBM)


def plan_kernel(lengths_ref, owners_ref, ids_ref, slots_ref, asked_ref):
    n_owners, capacity = asked_ref.shape
    n_rows = owners_ref.shape[0]
    owner_iota = lax.broadcasted_iota(jnp.int32, (n_owners, LANES), 0)
    slot_iota = lax.broadcasted_iota(jnp.int32, (capacity, LANES), 0)
    lane = lax.broadcasted_iota(jnp.int32, (1, LANES), 1)
    before = lax.broadcasted_iota(jnp.int32, (LANES, LANES), 0) < lax.broadcasted_iota(
        jnp.int32, (LANES, LANES), 1
    )
    counter = jnp.concatenate(
        [before.astype(jnp.float32), jnp.ones((LANES, LANES), jnp.float32)], axis=1
    ).astype(jnp.bfloat16)
    owner_rows = [owners_ref[row : row + 1, :] for row in range(n_rows)]
    live = [lane < lengths_ref[row] for row in range(n_rows)]
    hot = [
        ((owner_iota == owner_rows[row]) & live[row]).astype(jnp.float32) for row in range(n_rows)
    ]
    counts = jnp.dot(
        jnp.concatenate(hot, axis=0).astype(jnp.bfloat16),
        counter,
        preferred_element_type=jnp.float32,
    )
    named = jnp.zeros((n_owners, LANES), jnp.float32)
    placed, parts = [], []
    for row in range(n_rows):
        mine = counts[row * n_owners : (row + 1) * n_owners]
        slot = jnp.sum(hot[row] * (mine[:, :LANES] + named), axis=0, keepdims=True).astype(
            jnp.int32
        )
        named = named + mine[:, LANES:]
        slots_ref[row : row + 1, :] = jnp.where(live[row], owner_rows[row] * capacity + slot, 0)
        placed.append((slot_iota == slot).astype(jnp.float32).astype(jnp.bfloat16))
        ids_row = ids_ref[row : row + 1, :]
        parts.append(
            jnp.concatenate(
                [
                    hot[row] * (ids_row // LOW).astype(jnp.float32),
                    hot[row] * (ids_row % LOW).astype(jnp.float32),
                ],
                axis=0,
            ).astype(jnp.bfloat16)
        )
    both = lax.dot_general(
        jnp.concatenate(parts, axis=1),
        jnp.concatenate(placed, axis=1),
        (((1,), (1,)), ((), ())),
        preferred_element_type=jnp.float32,
    )
    ids = both[:n_owners].astype(jnp.int32) * LOW + both[n_owners:].astype(jnp.int32)
    first = lax.broadcasted_iota(jnp.int32, (n_owners, capacity), 1) == 0
    asked_ref[...] = ids + jnp.where(first, named[:, :capacity].astype(jnp.int32) * COUNT, 0)


def plan(lengths, owners, local_ids, n_owners, capacity):
    rows = owners.shape[0]
    return pl.pallas_call(
        plan_kernel,
        in_specs=[SMEM, VMEM, VMEM],
        out_specs=[VMEM, VMEM],
        out_shape=[
            jax.ShapeDtypeStruct((rows, LANES), jnp.int32),
            jax.ShapeDtypeStruct((n_owners, capacity), jnp.int32),
        ],
        name="plan",
    )(lengths, owners, local_ids)


def gather_kernel(asked_ref, table_ref, out_ref, table_f32, out_f32):
    n_owners, capacity = asked_ref.shape
    table_f32[...] = table_ref[...].astype(jnp.float32)

    def device(source, carry):
        groups = (asked_ref[source, 0] // COUNT + GROUP - 1) // GROUP

        def group(index, carry):
            start = index * GROUP
            for slot in range(GROUP):
                row = asked_ref[source, start + slot] % COUNT
                out_f32[pl.ds(source * capacity + start + slot, 1), :] = table_f32[
                    pl.ds(row, 1), :
                ]
            return carry

        return lax.fori_loop(0, groups, group, carry)

    lax.fori_loop(0, n_owners, device, 0)
    out_ref[...] = out_f32[...].astype(jnp.bfloat16)


def gather_rows(asked, table):
    rows = asked.shape[0] * asked.shape[1]
    width = table.shape[1]
    return pl.pallas_call(
        gather_kernel,
        in_specs=[SMEM, VMEM],
        out_specs=VMEM,
        out_shape=jax.ShapeDtypeStruct((rows, width), jnp.bfloat16),
        scratch_shapes=[
            pltpu.VMEM(table.shape, jnp.float32),
            pltpu.VMEM((rows, width), jnp.float32),
        ],
        compiler_params=pltpu.CompilerParams(vmem_limit_bytes=16 * 2**20),
        name="gather_rows",
    )(asked, table)


def finish_kernel(slots_ref, lengths_ref, first_ref, second_ref, centers_ref, out_ref, centers_f32, mine):
    centers_f32[...] = centers_ref[...].astype(jnp.float32)
    n_passages = out_ref.shape[0] // LEN
    split = first_ref.shape[0] // LEN

    def passage_rows(passage, carry):
        groups = (lengths_ref[passage] + GROUP - 1) // GROUP

        def group(index, carry):
            start = index * GROUP
            for position in range(GROUP):
                row = slots_ref[passage, start + position]
                mine[pl.ds(passage * LEN + start + position, 1), :] = centers_f32[
                    pl.ds(row, 1), :
                ]
            return carry

        return lax.fori_loop(0, groups, group, carry)

    lax.fori_loop(0, n_passages, passage_rows, 0)
    position = lax.broadcasted_iota(jnp.int32, (LEN, 1), 0)
    for passage in range(n_passages):
        at = slice(passage * LEN, (passage + 1) * LEN)
        if passage < split:
            embedded = first_ref[at, :]
        else:
            embedded = second_ref[(passage - split) * LEN : (passage - split + 1) * LEN, :]
        difference = embedded.astype(jnp.float32) - mine[at, :]
        total = jnp.sum(difference * difference, axis=1, keepdims=True)
        result = difference * lax.rsqrt(total + 1e-06)
        alive = position < lengths_ref[passage]
        out_ref[at, :] = jnp.where(alive, result, 0.0).astype(jnp.bfloat16)


def finish(slots, lengths, first, second, centers):
    rows = slots.shape[0] * slots.shape[1]
    width = centers.shape[1]
    return pl.pallas_call(
        finish_kernel,
        in_specs=[SMEM, SMEM, VMEM, VMEM, VMEM],
        out_specs=VMEM,
        out_shape=jax.ShapeDtypeStruct((rows, width), jnp.bfloat16),
        scratch_shapes=[
            pltpu.VMEM(centers.shape, jnp.float32),
            pltpu.VMEM((rows, width), jnp.float32),
        ],
        compiler_params=pltpu.CompilerParams(vmem_limit_bytes=16 * 2**20),
        name="finish",
    )(slots, lengths, first, second, centers)


def encode_kernel(
    start, chunk, rows_hbm, up_hbm, up_bias_hbm, down_hbm, down_bias_hbm, gain_hbm, shift_hbm, proj_hbm,
    out_ref, rows_vmem, up_vmem, up_bias, down_vmem, down_bias, gain, shift, proj,
    rows_in, weights_in, small_in,
):
    n_chunks = up_vmem.shape[0]
    tile_rows = rows_vmem.shape[1]
    tile_index = pl.program_id(0)

    def rows_copy(index):
        return pltpu.make_async_copy(
            rows_hbm.at[pl.ds(start + index * tile_rows, tile_rows), :],
            rows_vmem.at[index],
            rows_in.at[index],
        )

    def up_copy(index):
        return pltpu.make_async_copy(
            up_hbm.at[:, pl.ds(index * chunk, chunk)], up_vmem.at[index], weights_in.at[0, index]
        )

    def down_copy(index):
        return pltpu.make_async_copy(
            down_hbm.at[pl.ds(index * chunk, chunk), :], down_vmem.at[index], weights_in.at[1, index]
        )

    up_bias_copy = pltpu.make_async_copy(up_bias_hbm, up_bias, small_in.at[0])
    last_copies = [
        pltpu.make_async_copy(source, target, small_in.at[1 + index])
        for index, (source, target) in enumerate(
            [
                (down_bias_hbm, down_bias),
                (gain_hbm, gain),
                (shift_hbm, shift),
                (proj_hbm, proj),
            ]
        )
    ]

    queue = [down_copy(0)]
    for index in range(1, n_chunks):
        queue += [up_copy(index), down_copy(index)]
    queue += last_copies + [rows_copy(index) for index in range(1, rows_vmem.shape[0])]

    def start_next(done):
        for copy in queue[AHEAD + done : AHEAD + done + 1]:
            copy.start()

    def tile(first):
        rows = rows_vmem[tile_index]
        total = None
        for index in range(n_chunks):
            if first:
                up_copy(index).wait()
                start_next(2 * index)
            up_proj = (
                jnp.dot(rows, up_vmem[index], preferred_element_type=jnp.float32)
                + up_bias[index * chunk : (index + 1) * chunk][None, :]
            )
            activated = (0.5 * up_proj * (1.0 + lax.erf(up_proj * 0.7071067811865476))).astype(
                jnp.bfloat16
            )
            if first:
                down_copy(index).wait()
                start_next(2 * index + 1)
            part = jnp.dot(activated, down_vmem[index], preferred_element_type=jnp.float32)
            total = part if total is None else total + part
        if first:
            for copy in queue[AHEAD + 2 * n_chunks :]:
                copy.start()
            for copy in last_copies:
                copy.wait()
        ffn_out = total + down_bias[...][None, :] + rows.astype(jnp.float32)
        center = jnp.mean(ffn_out, axis=1, keepdims=True)
        centered = ffn_out - center
        spread = jnp.mean(centered * centered, axis=1, keepdims=True)
        normed = (
            centered * lax.rsqrt(spread + 1e-05) * gain[...][None, :] + shift[...][None, :]
        ).astype(jnp.bfloat16)
        projected = jnp.dot(normed, proj[...], preferred_element_type=jnp.float32)
        size = jnp.sum(projected * projected, axis=1, keepdims=True)
        out_ref[...] = (projected * lax.rsqrt(size + 1e-06)).astype(jnp.bfloat16)

    @pl.when(tile_index == 0)
    def _():
        rows_copy(0).start()
        up_copy(0).start()
        up_bias_copy.start()
        for copy in queue[:AHEAD]:
            copy.start()
        up_bias_copy.wait()
        rows_copy(0).wait()
        tile(True)

    @pl.when(tile_index > 0)
    def _():
        rows_copy(tile_index).wait()
        tile(False)


def encode(hidden_in, weights, start, rows, tile_rows, chunk):
    up_weight, up_bias, down_weight, down_bias, norm_gain, norm_shift, proj_weight = weights
    width, hidden = up_weight.shape
    out_width = proj_weight.shape[1]
    n_chunks = hidden // chunk
    n_tiles = rows // tile_rows
    return pl.pallas_call(
        functools.partial(encode_kernel, start, chunk),
        grid=(n_tiles,),
        in_specs=[HBM] * 8,
        out_specs=pl.BlockSpec((tile_rows, out_width), lambda index: (index, 0)),
        out_shape=jax.ShapeDtypeStruct((rows, out_width), jnp.bfloat16),
        scratch_shapes=[
            pltpu.VMEM((n_tiles, tile_rows, width), jnp.bfloat16),
            pltpu.VMEM((n_chunks, width, chunk), jnp.bfloat16),
            pltpu.VMEM(up_bias.shape, jnp.float32),
            pltpu.VMEM((n_chunks, chunk, width), jnp.bfloat16),
            pltpu.VMEM(down_bias.shape, jnp.float32),
            pltpu.VMEM(norm_gain.shape, jnp.float32),
            pltpu.VMEM(norm_shift.shape, jnp.float32),
            pltpu.VMEM(proj_weight.shape, jnp.bfloat16),
            pltpu.SemaphoreType.DMA((n_tiles,)),
            pltpu.SemaphoreType.DMA((2, n_chunks)),
            pltpu.SemaphoreType.DMA((5,)),
        ],
        compiler_params=pltpu.CompilerParams(vmem_limit_bytes=VMEM_BYTES),
        cost_estimate=pl.CostEstimate(
            flops=2 * rows * (2 * width * hidden + width * out_width),
            bytes_accessed=4 * width * hidden + 2 * rows * width,
            transcendentals=0,
        ),
        name="encode",
    )(hidden_in, up_weight, up_bias, down_weight, down_bias, norm_gain, norm_shift, proj_weight)


def body(
    hidden_in, up_weight, up_bias, down_weight, down_bias, norm_gain, norm_shift, proj_weight,
    centroids, lengths, owners, local_ids,
):
    n_devices = lax.axis_size("dp")
    token_rows = hidden_in.shape[0]
    width_out = proj_weight.shape[1]
    capacity = max(2, 2 * token_rows // n_devices)
    weights = (
        up_weight, up_bias, down_weight, down_bias, norm_gain, norm_shift, proj_weight,
    )
    early = token_rows // 4
    slots, asked = plan(
        lengths, owners.reshape(-1, LANES), local_ids.reshape(-1, LANES), n_devices, capacity
    )
    arrived = lax.all_to_all(asked, "dp", split_axis=0, concat_axis=0, tiled=True)
    first = encode(hidden_in, weights, 0, early, 256, 768)
    arrived, first = lax.optimization_barrier((arrived, first))
    rows = gather_rows(arrived, centroids)
    hidden_in, rows = lax.optimization_barrier((hidden_in, rows))
    centers = lax.all_to_all(
        rows.reshape(n_devices, capacity, width_out), "dp", split_axis=0, concat_axis=0, tiled=True
    )
    second = encode(hidden_in, weights, early, token_rows - early, 384, 768)
    centers, second = lax.optimization_barrier((centers, second))
    return finish(slots, lengths, first, second, centers.reshape(-1, width_out))


def solution(mesh):
    in_specs = (
        P(("groups", "dp"), None),
        P(),
        P(),
        P(),
        P(),
        P(),
        P(),
        P(),
        P("dp", None),
        P(("groups", "dp")),
        P(("groups", "dp"), None),
        P(("groups", "dp")),
    )
    out_specs = P(("groups", "dp"), None)
    return jax.shard_map(body, mesh=mesh, in_specs=in_specs, out_specs=out_specs, check_vma=False)
```

```python
import functools

import jax
import jax.numpy as jnp
from jax import lax
from jax.experimental import pallas as pl
from jax.experimental.pallas import tpu as pltpu
from jax.sharding import PartitionSpec as P

LEN = 128
LANES = 128
LOW_BITS = 6
LOW = 1 << LOW_BITS
COUNT_SHIFT = 16
BLOCK = 32
VMEM_BYTES = 16 * 2**20
ENC_BYTES = 48 * 2**20
AHEAD = 3
VMEM = pl.BlockSpec(memory_space=pltpu.VMEM)
SMEM = pl.BlockSpec(memory_space=pltpu.SMEM)
HBM = pl.BlockSpec(memory_space=pltpu.HBM)


def plan_kernel(lengths_ref, owners_ref, ids_ref, slots_ref, asked_ref):
    n_owners, capacity = asked_ref.shape
    n_rows = owners_ref.shape[0]
    owner_iota = lax.broadcasted_iota(jnp.int32, (n_owners, LANES), 0)
    slot_iota = lax.broadcasted_iota(jnp.int32, (capacity, LANES), 0)
    lane = lax.broadcasted_iota(jnp.int32, (1, LANES), 1)
    before = lax.broadcasted_iota(jnp.int32, (LANES, LANES), 0) < lax.broadcasted_iota(
        jnp.int32, (LANES, LANES), 1
    )
    counter = jnp.concatenate(
        [before.astype(jnp.float32), jnp.ones((LANES, LANES), jnp.float32)], axis=1
    ).astype(jnp.bfloat16)
    owner_rows = [owners_ref[row : row + 1, :] for row in range(n_rows)]
    live = [lane < lengths_ref[row] for row in range(n_rows)]
    hot = [
        ((owner_iota == owner_rows[row]) & live[row]).astype(jnp.float32) for row in range(n_rows)
    ]
    counts = jnp.dot(
        jnp.concatenate(hot, axis=0).astype(jnp.bfloat16),
        counter,
        preferred_element_type=jnp.float32,
    )
    named = jnp.zeros((n_owners, LANES), jnp.float32)
    placed, parts = [], []
    for row in range(n_rows):
        mine = counts[row * n_owners : (row + 1) * n_owners]
        slot = jnp.sum(hot[row] * (mine[:, :LANES] + named), axis=0, keepdims=True).astype(
            jnp.int32
        )
        named = named + mine[:, LANES:]
        slots_ref[n_rows + row : n_rows + row + 1, :] = jnp.full(
            (1, LANES), lengths_ref[row], jnp.int32
        )
        slots_ref[row : row + 1, :] = jnp.where(live[row], owner_rows[row] * capacity + slot, 0)
        placed.append((slot_iota == slot).astype(jnp.float32).astype(jnp.bfloat16))
        ids_row = ids_ref[row : row + 1, :]
        parts.append(
            jnp.concatenate(
                [
                    hot[row] * ((ids_row >> LOW_BITS)).astype(jnp.float32),
                    hot[row] * ((ids_row & (LOW - 1))).astype(jnp.float32),
                ],
                axis=0,
            ).astype(jnp.bfloat16)
        )
    both = lax.dot_general(
        jnp.concatenate(parts, axis=1),
        jnp.concatenate(placed, axis=1),
        (((1,), (1,)), ((), ())),
        preferred_element_type=jnp.float32,
    )
    ids = both[:n_owners].astype(jnp.int32) * LOW + both[n_owners:].astype(jnp.int32)
    first = lax.broadcasted_iota(jnp.int32, (n_owners, capacity), 1) == 0
    asked_ref[...] = ids + jnp.where(first, named[:, :capacity].astype(jnp.int32) << COUNT_SHIFT, 0)


def plan(lengths, owners, local_ids, n_owners, capacity):
    rows = owners.shape[0]
    return pl.pallas_call(
        plan_kernel,
        in_specs=[SMEM, VMEM, VMEM],
        out_specs=[VMEM, VMEM],
        out_shape=[
            jax.ShapeDtypeStruct((2 * rows, LANES), jnp.int32),
            jax.ShapeDtypeStruct((n_owners, capacity), jnp.int32),
        ],
        cost_estimate=pl.CostEstimate(flops=2 * 10**10, bytes_accessed=2**20, transcendentals=0),
        name="plan",
    )(lengths, owners, local_ids)


def gather_kernel(asked_ref, table_ref, out_ref, table_f32, out_f32):
    n_owners, capacity = asked_ref.shape
    table_f32[...] = table_ref[...].astype(jnp.float32)

    block = min(BLOCK, capacity)

    def device(source, carry):
        count = asked_ref[source, 0] >> COUNT_SHIFT
        base = source * capacity
        for start in range(0, capacity, block):

            @pl.when(count > start)
            def _():
                for slot in range(start, start + block):
                    row = asked_ref[source, slot]
                    if slot == 0:
                        row = row & ((1 << COUNT_SHIFT) - 1)
                    out_f32[pl.ds(base + slot, 1), :] = table_f32[pl.ds(row, 1), :]

        return carry

    lax.fori_loop(0, n_owners, device, 0)
    out_ref[...] = out_f32[...].astype(jnp.bfloat16)


def gather_rows(asked, table):
    rows = asked.shape[0] * asked.shape[1]
    width = table.shape[1]
    return pl.pallas_call(
        gather_kernel,
        in_specs=[SMEM, VMEM],
        out_specs=VMEM,
        out_shape=jax.ShapeDtypeStruct((rows, width), jnp.bfloat16),
        scratch_shapes=[
            pltpu.VMEM(table.shape, jnp.float32),
            pltpu.VMEM((rows, width), jnp.float32),
        ],
        compiler_params=pltpu.CompilerParams(vmem_limit_bytes=VMEM_BYTES),
        cost_estimate=pl.CostEstimate(flops=2 * 10**10, bytes_accessed=2**20, transcendentals=0),
        name="gather_rows",
    )(asked, table)


def finish_kernel(slots_ref, embedded_ref, centers_ref, out_ref, centers_f32, mine):
    centers_f32[...] = centers_ref[...].astype(jnp.float32)
    n_passages = out_ref.shape[0] // LEN

    def passage_rows(passage, carry):
        length = slots_ref[n_passages + passage, 0]
        base = passage * LEN
        for start in range(0, LEN, BLOCK):

            @pl.when(length > start)
            def _():
                for position in range(start, start + BLOCK):
                    row = slots_ref[passage, position]
                    mine[pl.ds(base + position, 1), :] = centers_f32[pl.ds(row, 1), :]

        return carry

    lax.fori_loop(0, n_passages, passage_rows, 0)
    position = lax.broadcasted_iota(jnp.int32, (LEN, 1), 0)
    for passage in range(n_passages):
        at = slice(passage * LEN, (passage + 1) * LEN)
        difference = embedded_ref[at, :].astype(jnp.float32) - mine[at, :]
        total = jnp.sum(difference * difference, axis=1, keepdims=True)
        result = difference * lax.rsqrt(total + 1e-06)
        alive = position < slots_ref[n_passages + passage, 0]
        out_ref[at, :] = jnp.where(alive, result, 0.0).astype(jnp.bfloat16)


def finish(slots, embedded, centers):
    rows = embedded.shape[0]
    width = centers.shape[1]
    return pl.pallas_call(
        finish_kernel,
        in_specs=[SMEM, VMEM, VMEM],
        out_specs=VMEM,
        out_shape=jax.ShapeDtypeStruct((rows, width), jnp.bfloat16),
        scratch_shapes=[
            pltpu.VMEM(centers.shape, jnp.float32),
            pltpu.VMEM((rows, width), jnp.float32),
        ],
        compiler_params=pltpu.CompilerParams(vmem_limit_bytes=VMEM_BYTES),
        name="finish",
    )(slots, embedded, centers)


def encode_kernel(
    tile_rows, chunk, rows_ref, up_hbm, up_bias, down_hbm, down_bias, gain, shift, proj, out_ref,
    up_vmem, down_vmem, arrived,
):
    n_chunks = up_vmem.shape[0]
    queue = []
    for index in range(n_chunks):
        at = pl.ds(index * chunk, chunk)
        queue += [
            pltpu.make_async_copy(up_hbm.at[:, at], up_vmem.at[index], arrived.at[2 * index]),
            pltpu.make_async_copy(
                down_hbm.at[at, :], down_vmem.at[index], arrived.at[2 * index + 1]
            ),
        ]

    def wait_weights(index):
        queue[index].wait()
        for copy in queue[index + AHEAD : index + AHEAD + 1]:
            copy.start()

    def tile(start, first):
        at = pl.ds(start, tile_rows)
        rows = rows_ref[at, :]

        def up(index):
            return (
                jnp.dot(rows, up_vmem[index], preferred_element_type=jnp.float32)
                + up_bias[index * chunk : (index + 1) * chunk][None, :]
            )

        total = None
        if first:
            wait_weights(0)
        up_proj = up(0)
        for index in range(n_chunks):
            if first:
                wait_weights(2 * index + 1)
                if index + 1 < n_chunks:
                    wait_weights(2 * index + 2)
            following = up(index + 1) if first and index + 1 < n_chunks else None
            if not first and index > 0:
                up_proj = up(index)
            activated = (0.5 * up_proj * (1.0 + lax.erf(up_proj * 0.7071067811865476))).astype(
                jnp.bfloat16
            )
            part = jnp.dot(activated, down_vmem[index], preferred_element_type=jnp.float32)
            total = part if total is None else total + part
            up_proj = following
        ffn_out = total + down_bias[...][None, :] + rows.astype(jnp.float32)
        center = jnp.mean(ffn_out, axis=1, keepdims=True)
        centered = ffn_out - center
        spread = jnp.mean(centered * centered, axis=1, keepdims=True)
        normed = (
            centered * lax.rsqrt(spread + 1e-05) * gain[...][None, :] + shift[...][None, :]
        ).astype(jnp.bfloat16)
        projected = jnp.dot(normed, proj[...], preferred_element_type=jnp.float32)
        size = jnp.sum(projected * projected, axis=1, keepdims=True)
        out_ref[at, :] = (projected * lax.rsqrt(size + 1e-06)).astype(jnp.bfloat16)

    for copy in queue[:AHEAD]:
        copy.start()
    tile(0, True)

    def later(index, carry):
        tile(pl.multiple_of(index * tile_rows, tile_rows), False)
        return carry

    lax.fori_loop(1, out_ref.shape[0] // tile_rows, later, 0)


def encode(hidden_in, weights, start, rows, tile_rows, chunk):
    up_weight, up_bias, down_weight, down_bias, norm_gain, norm_shift, proj_weight = weights
    width, hidden = up_weight.shape
    out_width = proj_weight.shape[1]
    n_chunks = hidden // chunk
    return pl.pallas_call(
        functools.partial(encode_kernel, tile_rows, chunk),
        in_specs=[VMEM, HBM, VMEM, HBM, VMEM, VMEM, VMEM, VMEM],
        out_specs=VMEM,
        out_shape=jax.ShapeDtypeStruct((rows, out_width), jnp.bfloat16),
        scratch_shapes=[
            pltpu.VMEM((n_chunks, width, chunk), jnp.bfloat16),
            pltpu.VMEM((n_chunks, chunk, width), jnp.bfloat16),
            pltpu.SemaphoreType.DMA((2 * n_chunks,)),
        ],
        compiler_params=pltpu.CompilerParams(vmem_limit_bytes=ENC_BYTES),
        cost_estimate=pl.CostEstimate(
            flops=2 * rows * (2 * width * hidden + width * out_width),
            bytes_accessed=4 * width * hidden + 2 * rows * width,
            transcendentals=0,
        ),
        name="encode",
    )(hidden_in, up_weight, up_bias, down_weight, down_bias, norm_gain, norm_shift, proj_weight)


def body(
    hidden_in, up_weight, up_bias, down_weight, down_bias, norm_gain, norm_shift, proj_weight,
    centroids, lengths, owners, local_ids,
):
    n_devices = lax.axis_size("dp")
    token_rows = hidden_in.shape[0]
    width_out = proj_weight.shape[1]
    capacity = max(2, 2 * token_rows // n_devices)
    weights = (
        up_weight, up_bias, down_weight, down_bias, norm_gain, norm_shift, proj_weight,
    )
    slots, asked = plan(
        lengths, owners.reshape(-1, LANES), local_ids.reshape(-1, LANES), n_devices, capacity
    )
    arrived = lax.all_to_all(asked, "dp", split_axis=0, concat_axis=0, tiled=True)
    rows = gather_rows(arrived, centroids)
    hidden_in, rows = lax.optimization_barrier((hidden_in, rows))
    centers = lax.all_to_all(
        rows.reshape(n_devices, capacity, width_out), "dp", split_axis=0, concat_axis=0, tiled=True
    )
    embedded = encode(hidden_in, weights, 0, token_rows, 512, 768)
    centers, embedded = lax.optimization_barrier((centers, embedded))
    return finish(slots, embedded, centers.reshape(-1, width_out))


def solution(mesh):
    in_specs = (
        P(("groups", "dp"), None),
        P(),
        P(),
        P(),
        P(),
        P(),
        P(),
        P(),
        P("dp", None),
        P(("groups", "dp")),
        P(("groups", "dp"), None),
        P(("groups", "dp")),
    )
    out_specs = P(("groups", "dp"), None)
    return jax.shard_map(body, mesh=mesh, in_specs=in_specs, out_specs=out_specs, check_vma=False)
```

```python
import functools

import jax
import jax.numpy as jnp
from jax import lax
from jax.experimental import pallas as pl
from jax.experimental.pallas import tpu as pltpu
from jax.sharding import PartitionSpec as P

LEN = 128
LANES = 128
LOW_BITS = 6
LOW = 1 << LOW_BITS
COUNT_SHIFT = 16
BLOCK = 32
VMEM_BYTES = 16 * 2**20
ENC_BYTES = 53 * 2**20
AHEAD = 3
VMEM = pl.BlockSpec(memory_space=pltpu.VMEM)
SMEM = pl.BlockSpec(memory_space=pltpu.SMEM)
HBM = pl.BlockSpec(memory_space=pltpu.HBM)
ANY = pl.BlockSpec(memory_space=pl.ANY)


def plan_kernel(lengths_ref, owners_ref, ids_ref, slots_ref, asked_ref):
    n_owners, capacity = asked_ref.shape
    n_rows = owners_ref.shape[0]
    owner_iota = lax.broadcasted_iota(jnp.int32, (n_owners, LANES), 0)
    slot_iota = lax.broadcasted_iota(jnp.int32, (capacity, LANES), 0)
    lane = lax.broadcasted_iota(jnp.int32, (1, LANES), 1)
    before = lax.broadcasted_iota(jnp.int32, (LANES, LANES), 0) < lax.broadcasted_iota(
        jnp.int32, (LANES, LANES), 1
    )
    counter = jnp.concatenate(
        [before.astype(jnp.float32), jnp.ones((LANES, LANES), jnp.float32)], axis=1
    ).astype(jnp.bfloat16)
    owner_rows = [owners_ref[row : row + 1, :] for row in range(n_rows)]
    live = [lane < lengths_ref[row] for row in range(n_rows)]
    hot = [
        ((owner_iota == owner_rows[row]) & live[row]).astype(jnp.float32) for row in range(n_rows)
    ]
    counts = jnp.dot(
        jnp.concatenate(hot, axis=0).astype(jnp.bfloat16),
        counter,
        preferred_element_type=jnp.float32,
    )
    named = jnp.zeros((n_owners, LANES), jnp.float32)
    placed, parts = [], []
    for row in range(n_rows):
        mine = counts[row * n_owners : (row + 1) * n_owners]
        slot = jnp.sum(hot[row] * (mine[:, :LANES] + named), axis=0, keepdims=True).astype(
            jnp.int32
        )
        named = named + mine[:, LANES:]
        slots_ref[n_rows + row : n_rows + row + 1, :] = jnp.full(
            (1, LANES), lengths_ref[row], jnp.int32
        )
        slots_ref[row : row + 1, :] = jnp.where(live[row], owner_rows[row] * capacity + slot, 0)
        placed.append((slot_iota == slot).astype(jnp.float32).astype(jnp.bfloat16))
        ids_row = ids_ref[row : row + 1, :]
        parts.append(
            jnp.concatenate(
                [
                    hot[row] * ((ids_row >> LOW_BITS)).astype(jnp.float32),
                    hot[row] * ((ids_row & (LOW - 1))).astype(jnp.float32),
                ],
                axis=0,
            ).astype(jnp.bfloat16)
        )
    both = lax.dot_general(
        jnp.concatenate(parts, axis=1),
        jnp.concatenate(placed, axis=1),
        (((1,), (1,)), ((), ())),
        preferred_element_type=jnp.float32,
    )
    ids = both[:n_owners].astype(jnp.int32) * LOW + both[n_owners:].astype(jnp.int32)
    first = lax.broadcasted_iota(jnp.int32, (n_owners, capacity), 1) == 0
    asked_ref[...] = ids + jnp.where(first, named[:, :capacity].astype(jnp.int32) << COUNT_SHIFT, 0)


def plan(lengths, owners, local_ids, n_owners, capacity):
    rows = owners.shape[0]
    return pl.pallas_call(
        plan_kernel,
        in_specs=[SMEM, VMEM, VMEM],
        out_specs=[VMEM, VMEM],
        out_shape=[
            jax.ShapeDtypeStruct((2 * rows, LANES), jnp.int32),
            jax.ShapeDtypeStruct((n_owners, capacity), jnp.int32),
        ],
        cost_estimate=pl.CostEstimate(flops=2 * 10**10, bytes_accessed=2**20, transcendentals=0),
        name="plan",
    )(lengths, owners, local_ids)


def gather_kernel(asked_hbm, table_ref, out_ref, asked_ref, table_f32, out_f32, arrived):
    n_owners, capacity = asked_ref.shape
    asked_copy = pltpu.make_async_copy(asked_hbm, asked_ref, arrived)
    asked_copy.start()
    table_f32[...] = table_ref[...].astype(jnp.float32)

    block = min(BLOCK, capacity)

    def device(source, carry):
        count = asked_ref[source, 0] >> COUNT_SHIFT
        base = source * capacity
        for start in range(0, capacity, block):

            @pl.when(count > start)
            def _():
                for slot in range(start, start + block):
                    row = asked_ref[source, slot]
                    if slot == 0:
                        row = row & ((1 << COUNT_SHIFT) - 1)
                    out_f32[pl.ds(base + slot, 1), :] = table_f32[pl.ds(row, 1), :]

        return carry

    asked_copy.wait()
    lax.fori_loop(0, n_owners, device, 0)
    out_ref[...] = out_f32[...].astype(jnp.bfloat16)


def gather_rows(asked, table):
    rows = asked.shape[0] * asked.shape[1]
    width = table.shape[1]
    return pl.pallas_call(
        gather_kernel,
        in_specs=[ANY, VMEM],
        out_specs=VMEM,
        out_shape=jax.ShapeDtypeStruct((rows, width), jnp.bfloat16),
        scratch_shapes=[
            pltpu.SMEM(asked.shape, jnp.int32),
            pltpu.VMEM(table.shape, jnp.float32),
            pltpu.VMEM((rows, width), jnp.float32),
            pltpu.SemaphoreType.DMA,
        ],
        compiler_params=pltpu.CompilerParams(vmem_limit_bytes=VMEM_BYTES),
        cost_estimate=pl.CostEstimate(flops=2 * 10**10, bytes_accessed=2**20, transcendentals=0),
        name="gather_rows",
    )(asked, table)


def finish_kernel(
    slots_hbm, embedded_ref, centers_ref, out_ref, slots_ref, centers_f32, mine, arrived
):
    slots_copy = pltpu.make_async_copy(slots_hbm, slots_ref, arrived)
    slots_copy.start()
    centers_f32[...] = centers_ref[...].astype(jnp.float32)
    n_passages = out_ref.shape[0] // LEN

    def passage_rows(passage, carry):
        length = slots_ref[n_passages + passage, 0]
        base = passage * LEN
        for start in range(0, LEN, BLOCK):

            @pl.when(length > start)
            def _():
                for position in range(start, start + BLOCK):
                    row = slots_ref[passage, position]
                    mine[pl.ds(base + position, 1), :] = centers_f32[pl.ds(row, 1), :]

        return carry

    slots_copy.wait()
    lax.fori_loop(0, n_passages, passage_rows, 0)
    position = lax.broadcasted_iota(jnp.int32, (LEN, 1), 0)
    for passage in range(n_passages):
        at = slice(passage * LEN, (passage + 1) * LEN)
        difference = embedded_ref[at, :].astype(jnp.float32) - mine[at, :]
        total = jnp.sum(difference * difference, axis=1, keepdims=True)
        result = difference * lax.rsqrt(total + 1e-06)
        alive = position < slots_ref[n_passages + passage, 0]
        out_ref[at, :] = jnp.where(alive, result, 0.0).astype(jnp.bfloat16)


def finish(slots, embedded, centers):
    rows = embedded.shape[0]
    width = centers.shape[1]
    return pl.pallas_call(
        finish_kernel,
        in_specs=[ANY, VMEM, VMEM],
        out_specs=VMEM,
        out_shape=jax.ShapeDtypeStruct((rows, width), jnp.bfloat16),
        scratch_shapes=[
            pltpu.SMEM(slots.shape, jnp.int32),
            pltpu.VMEM(centers.shape, jnp.float32),
            pltpu.VMEM((rows, width), jnp.float32),
            pltpu.SemaphoreType.DMA,
        ],
        compiler_params=pltpu.CompilerParams(vmem_limit_bytes=VMEM_BYTES),
        name="finish",
    )(slots, embedded, centers)


def encode_kernel(
    first_rows, later_rows, chunk, rows_hbm, up_hbm, up_bias, down_hbm, down_bias, gain, shift, proj, out_ref,
    rows_vmem, up_vmem, down_vmem, arrived,
):
    n_chunks = up_vmem.shape[0]
    queue = []
    for index in range(n_chunks):
        at = pl.ds(index * chunk, chunk)
        queue += [
            pltpu.make_async_copy(up_hbm.at[:, at], up_vmem.at[index], arrived.at[2 * index]),
            pltpu.make_async_copy(
                down_hbm.at[at, :], down_vmem.at[index], arrived.at[2 * index + 1]
            ),
        ]

    def rows_copy(start, count, semaphore):
        at = pl.ds(start, count)
        return pltpu.make_async_copy(rows_hbm.at[at, :], rows_vmem.at[at, :], semaphore)

    n_rows = out_ref.shape[0]
    rows_first = rows_copy(0, first_rows, arrived.at[2 * n_chunks])
    queue.append(rows_copy(first_rows, n_rows - first_rows, arrived.at[2 * n_chunks + 1]))

    def wait_weights(index):
        queue[index].wait()
        for copy in queue[index + AHEAD : index + AHEAD + 1]:
            copy.start()

    def tile(start, count, first):
        at = pl.ds(start, count)
        rows = rows_vmem[at, :]

        def up(index):
            return (
                jnp.dot(rows, up_vmem[index], preferred_element_type=jnp.float32)
                + up_bias[index * chunk : (index + 1) * chunk][None, :]
            )

        total = None
        if first:
            wait_weights(0)
        up_proj = up(0)
        for index in range(n_chunks):
            if first:
                wait_weights(2 * index + 1)
                if index + 1 < n_chunks:
                    wait_weights(2 * index + 2)
            following = up(index + 1) if first and index + 1 < n_chunks else None
            if not first and index > 0:
                up_proj = up(index)
            activated = (0.5 * up_proj * (1.0 + lax.erf(up_proj * 0.7071067811865476))).astype(
                jnp.bfloat16
            )
            part = jnp.dot(activated, down_vmem[index], preferred_element_type=jnp.float32)
            total = part if total is None else total + part
            up_proj = following
        ffn_out = total + down_bias[...][None, :] + rows.astype(jnp.float32)
        center = jnp.mean(ffn_out, axis=1, keepdims=True)
        centered = ffn_out - center
        spread = jnp.mean(centered * centered, axis=1, keepdims=True)
        normed = (
            centered * lax.rsqrt(spread + 1e-05) * gain[...][None, :] + shift[...][None, :]
        ).astype(jnp.bfloat16)
        projected = jnp.dot(normed, proj[...], preferred_element_type=jnp.float32)
        size = jnp.sum(projected * projected, axis=1, keepdims=True)
        out_ref[at, :] = (projected * lax.rsqrt(size + 1e-06)).astype(jnp.bfloat16)

    rows_first.start()
    for copy in queue[:AHEAD]:
        copy.start()
    rows_first.wait()
    tile(0, first_rows, True)
    wait_weights(2 * n_chunks)

    def later(index, carry):
        start = pl.multiple_of(first_rows + index * later_rows, LANES)
        tile(start, later_rows, False)
        return carry

    lax.fori_loop(0, (n_rows - first_rows) // later_rows, later, 0)


def encode(hidden_in, weights, first_rows, later_rows, chunk):
    rows = hidden_in.shape[0]
    up_weight, up_bias, down_weight, down_bias, norm_gain, norm_shift, proj_weight = weights
    width, hidden = up_weight.shape
    out_width = proj_weight.shape[1]
    n_chunks = hidden // chunk
    return pl.pallas_call(
        functools.partial(encode_kernel, first_rows, later_rows, chunk),
        in_specs=[HBM, HBM, VMEM, HBM, VMEM, VMEM, VMEM, VMEM],
        out_specs=VMEM,
        out_shape=jax.ShapeDtypeStruct((rows, out_width), jnp.bfloat16),
        scratch_shapes=[
            pltpu.VMEM((rows, width), jnp.bfloat16),
            pltpu.VMEM((n_chunks, width, chunk), jnp.bfloat16),
            pltpu.VMEM((n_chunks, chunk, width), jnp.bfloat16),
            pltpu.SemaphoreType.DMA((2 * n_chunks + 2,)),
        ],
        compiler_params=pltpu.CompilerParams(vmem_limit_bytes=ENC_BYTES),
        cost_estimate=pl.CostEstimate(
            flops=2 * rows * (2 * width * hidden + width * out_width),
            bytes_accessed=4 * width * hidden + 2 * rows * width,
            transcendentals=0,
        ),
        name="encode",
    )(hidden_in, up_weight, up_bias, down_weight, down_bias, norm_gain, norm_shift, proj_weight)


def body(
    hidden_in, up_weight, up_bias, down_weight, down_bias, norm_gain, norm_shift, proj_weight,
    centroids, lengths, owners, local_ids,
):
    n_devices = lax.axis_size("dp")
    token_rows = hidden_in.shape[0]
    width_out = proj_weight.shape[1]
    capacity = max(2, 2 * token_rows // n_devices)
    weights = (
        up_weight, up_bias, down_weight, down_bias, norm_gain, norm_shift, proj_weight,
    )
    slots, asked = plan(
        lengths, owners.reshape(-1, LANES), local_ids.reshape(-1, LANES), n_devices, capacity
    )
    arrived = lax.all_to_all(asked, "dp", split_axis=0, concat_axis=0, tiled=True)
    rows = gather_rows(arrived, centroids)
    hidden_in, rows = lax.optimization_barrier((hidden_in, rows))
    centers = lax.all_to_all(
        rows.reshape(n_devices, capacity, width_out), "dp", split_axis=0, concat_axis=0, tiled=True
    )
    embedded = encode(hidden_in, weights, 256, 768, 768)
    centers, embedded = lax.optimization_barrier((centers, embedded))
    return finish(slots, embedded, centers.reshape(-1, width_out))


def solution(mesh):
    in_specs = (
        P(("groups", "dp"), None),
        P(),
        P(),
        P(),
        P(),
        P(),
        P(),
        P(),
        P("dp", None),
        P(("groups", "dp")),
        P(("groups", "dp"), None),
        P(("groups", "dp")),
    )
    out_specs = P(("groups", "dp"), None)
    return jax.shard_map(body, mesh=mesh, in_specs=in_specs, out_specs=out_specs, check_vma=False)
```

```python
import functools

import jax
import jax.numpy as jnp
from jax import lax
from jax.experimental import pallas as pl
from jax.experimental.pallas import tpu as pltpu
from jax.sharding import PartitionSpec as P

LEN = 128
LANES = 128
LOW_BITS = 6
LOW = 1 << LOW_BITS
COUNT_SHIFT = 16
BLOCK = 32
VMEM_BYTES = 16 * 2**20
ENC_BYTES = 53 * 2**20
AHEAD = 10
FIRST_CHUNK = 256
VMEM = pl.BlockSpec(memory_space=pltpu.VMEM)
SMEM = pl.BlockSpec(memory_space=pltpu.SMEM)
HBM = pl.BlockSpec(memory_space=pltpu.HBM)
ANY = pl.BlockSpec(memory_space=pl.ANY)


def plan_kernel(lengths_ref, owners_ref, ids_ref, slots_ref, asked_ref):
    n_owners, capacity = asked_ref.shape
    n_rows = owners_ref.shape[0]
    owner_iota = lax.broadcasted_iota(jnp.int32, (n_owners, LANES), 0)
    slot_iota = lax.broadcasted_iota(jnp.int32, (capacity, LANES), 0)
    lane = lax.broadcasted_iota(jnp.int32, (1, LANES), 1)
    before = lax.broadcasted_iota(jnp.int32, (LANES, LANES), 0) < lax.broadcasted_iota(
        jnp.int32, (LANES, LANES), 1
    )
    counter = jnp.concatenate(
        [before.astype(jnp.float32), jnp.ones((LANES, LANES), jnp.float32)], axis=1
    ).astype(jnp.bfloat16)
    owner_rows = [owners_ref[row : row + 1, :] for row in range(n_rows)]
    live = [lane < lengths_ref[row] for row in range(n_rows)]
    hot = [
        ((owner_iota == owner_rows[row]) & live[row]).astype(jnp.float32) for row in range(n_rows)
    ]
    counts = jnp.dot(
        jnp.concatenate(hot, axis=0).astype(jnp.bfloat16),
        counter,
        preferred_element_type=jnp.float32,
    )
    named = jnp.zeros((n_owners, LANES), jnp.float32)
    placed, parts = [], []
    for row in range(n_rows):
        mine = counts[row * n_owners : (row + 1) * n_owners]
        slot = jnp.sum(hot[row] * (mine[:, :LANES] + named), axis=0, keepdims=True).astype(
            jnp.int32
        )
        named = named + mine[:, LANES:]
        slots_ref[n_rows + row : n_rows + row + 1, :] = jnp.full(
            (1, LANES), lengths_ref[row], jnp.int32
        )
        slots_ref[row : row + 1, :] = jnp.where(live[row], owner_rows[row] * capacity + slot, 0)
        placed.append((slot_iota == slot).astype(jnp.float32).astype(jnp.bfloat16))
        ids_row = ids_ref[row : row + 1, :]
        parts.append(
            jnp.concatenate(
                [
                    hot[row] * ((ids_row >> LOW_BITS)).astype(jnp.float32),
                    hot[row] * ((ids_row & (LOW - 1))).astype(jnp.float32),
                ],
                axis=0,
            ).astype(jnp.bfloat16)
        )
    both = lax.dot_general(
        jnp.concatenate(parts, axis=1),
        jnp.concatenate(placed, axis=1),
        (((1,), (1,)), ((), ())),
        preferred_element_type=jnp.float32,
    )
    ids = both[:n_owners].astype(jnp.int32) * LOW + both[n_owners:].astype(jnp.int32)
    first = lax.broadcasted_iota(jnp.int32, (n_owners, capacity), 1) == 0
    asked_ref[...] = ids + jnp.where(first, named[:, :capacity].astype(jnp.int32) << COUNT_SHIFT, 0)


def plan(lengths, owners, local_ids, n_owners, capacity):
    rows = owners.shape[0]
    return pl.pallas_call(
        plan_kernel,
        in_specs=[SMEM, VMEM, VMEM],
        out_specs=[VMEM, VMEM],
        out_shape=[
            jax.ShapeDtypeStruct((2 * rows, LANES), jnp.int32),
            jax.ShapeDtypeStruct((n_owners, capacity), jnp.int32),
        ],
        cost_estimate=pl.CostEstimate(flops=2 * 10**10, bytes_accessed=2**20, transcendentals=0),
        name="plan",
    )(lengths, owners, local_ids)


def gather_kernel(asked_hbm, table_ref, out_ref, asked_ref, table_f32, out_f32, arrived):
    n_owners, capacity = asked_ref.shape
    asked_copy = pltpu.make_async_copy(asked_hbm, asked_ref, arrived)
    asked_copy.start()
    table_f32[...] = table_ref[...].astype(jnp.float32)

    block = min(BLOCK, capacity)

    def device(source, carry):
        count = asked_ref[source, 0] >> COUNT_SHIFT
        base = source * capacity
        for start in range(0, capacity, block):

            @pl.when(count > start)
            def _():
                for slot in range(start, start + block):
                    row = asked_ref[source, slot]
                    if slot == 0:
                        row = row & ((1 << COUNT_SHIFT) - 1)
                    out_f32[pl.ds(base + slot, 1), :] = table_f32[pl.ds(row, 1), :]

        return carry

    asked_copy.wait()
    lax.fori_loop(0, n_owners, device, 0)
    out_ref[...] = out_f32[...].astype(jnp.bfloat16)


def gather_rows(asked, table):
    rows = asked.shape[0] * asked.shape[1]
    width = table.shape[1]
    return pl.pallas_call(
        gather_kernel,
        in_specs=[ANY, VMEM],
        out_specs=VMEM,
        out_shape=jax.ShapeDtypeStruct((rows, width), jnp.bfloat16),
        scratch_shapes=[
            pltpu.SMEM(asked.shape, jnp.int32),
            pltpu.VMEM(table.shape, jnp.float32),
            pltpu.VMEM((rows, width), jnp.float32),
            pltpu.SemaphoreType.DMA,
        ],
        compiler_params=pltpu.CompilerParams(vmem_limit_bytes=VMEM_BYTES),
        cost_estimate=pl.CostEstimate(flops=2 * 10**10, bytes_accessed=2**20, transcendentals=0),
        name="gather_rows",
    )(asked, table)


def finish_kernel(
    slots_hbm, embedded_ref, centers_ref, out_ref, slots_ref, centers_f32, mine, arrived
):
    slots_copy = pltpu.make_async_copy(slots_hbm, slots_ref, arrived)
    slots_copy.start()
    centers_f32[...] = centers_ref[...].astype(jnp.float32)
    n_passages = out_ref.shape[0] // LEN

    def passage_rows(passage, carry):
        length = slots_ref[n_passages + passage, 0]
        base = passage * LEN
        for start in range(0, LEN, BLOCK):

            @pl.when(length > start)
            def _():
                for position in range(start, start + BLOCK):
                    row = slots_ref[passage, position]
                    mine[pl.ds(base + position, 1), :] = centers_f32[pl.ds(row, 1), :]

        return carry

    slots_copy.wait()
    lax.fori_loop(0, n_passages, passage_rows, 0)
    position = lax.broadcasted_iota(jnp.int32, (LEN, 1), 0)
    for passage in range(n_passages):
        at = slice(passage * LEN, (passage + 1) * LEN)
        difference = embedded_ref[at, :].astype(jnp.float32) - mine[at, :]
        total = jnp.sum(difference * difference, axis=1, keepdims=True)
        result = difference * lax.rsqrt(total + 1e-06)
        alive = position < slots_ref[n_passages + passage, 0]
        out_ref[at, :] = jnp.where(alive, result, 0.0).astype(jnp.bfloat16)


def finish(slots, embedded, centers):
    rows = embedded.shape[0]
    width = centers.shape[1]
    return pl.pallas_call(
        finish_kernel,
        in_specs=[ANY, VMEM, VMEM],
        out_specs=VMEM,
        out_shape=jax.ShapeDtypeStruct((rows, width), jnp.bfloat16),
        scratch_shapes=[
            pltpu.SMEM(slots.shape, jnp.int32),
            pltpu.VMEM(centers.shape, jnp.float32),
            pltpu.VMEM((rows, width), jnp.float32),
            pltpu.SemaphoreType.DMA,
        ],
        compiler_params=pltpu.CompilerParams(vmem_limit_bytes=VMEM_BYTES),
        name="finish",
    )(slots, embedded, centers)


def encode_kernel(
    first_rows, later_rows, chunk, rows_hbm, up_hbm, up_bias, down_hbm, down_bias, gain, shift, proj, out_ref,
    rows_vmem, up_vmem, down_vmem, arrived,
):
    hidden = up_vmem.shape[1]
    later_bounds = list(range(0, hidden + 1, chunk))
    first_bounds = [0, FIRST_CHUNK] + later_bounds[1:]
    n_copies = 2 * (len(first_bounds) - 1)
    queue = []
    for low, high in zip(first_bounds, first_bounds[1:]):
        at = pl.ds(low, high - low)
        semaphores = [arrived.at[len(queue)], arrived.at[len(queue) + 1]]
        queue += [
            pltpu.make_async_copy(up_hbm.at[:, at], up_vmem.at[:, at], semaphores[0]),
            pltpu.make_async_copy(down_hbm.at[at, :], down_vmem.at[at, :], semaphores[1]),
        ]

    def rows_copy(start, count, semaphore):
        at = pl.ds(start, count)
        return pltpu.make_async_copy(rows_hbm.at[at, :], rows_vmem.at[at, :], semaphore)

    n_rows = out_ref.shape[0]
    rows_first = rows_copy(0, first_rows, arrived.at[n_copies])
    queue.append(rows_copy(first_rows, n_rows - first_rows, arrived.at[n_copies + 1]))

    def wait_weights(index):
        queue[index].wait()
        for copy in queue[index + AHEAD : index + AHEAD + 1]:
            copy.start()

    def tile(start, count, first):
        at = pl.ds(start, count)
        rows = rows_vmem[at, :]

        bounds = first_bounds if first else later_bounds
        n_chunks = len(bounds) - 1

        def up(index):
            part = slice(bounds[index], bounds[index + 1])
            return (
                jnp.dot(rows, up_vmem[:, part], preferred_element_type=jnp.float32)
                + up_bias[part][None, :]
            )

        total = None
        if first:
            wait_weights(0)
        up_proj = up(0)
        for index in range(n_chunks):
            if first:
                wait_weights(2 * index + 1)
                if index + 1 < n_chunks:
                    wait_weights(2 * index + 2)
            following = up(index + 1) if first and index + 1 < n_chunks else None
            if not first and index > 0:
                up_proj = up(index)
            activated = (0.5 * up_proj * (1.0 + lax.erf(up_proj * 0.7071067811865476))).astype(
                jnp.bfloat16
            )
            part = jnp.dot(
                activated,
                down_vmem[bounds[index] : bounds[index + 1], :],
                preferred_element_type=jnp.float32,
            )
            total = part if total is None else total + part
            up_proj = following
        ffn_out = total + down_bias[...][None, :] + rows.astype(jnp.float32)
        center = jnp.mean(ffn_out, axis=1, keepdims=True)
        centered = ffn_out - center
        spread = jnp.mean(centered * centered, axis=1, keepdims=True)
        normed = (
            centered * lax.rsqrt(spread + 1e-05) * gain[...][None, :] + shift[...][None, :]
        ).astype(jnp.bfloat16)
        projected = jnp.dot(normed, proj[...], preferred_element_type=jnp.float32)
        size = jnp.sum(projected * projected, axis=1, keepdims=True)
        out_ref[at, :] = (projected * lax.rsqrt(size + 1e-06)).astype(jnp.bfloat16)

    rows_first.start()
    for copy in queue[:AHEAD]:
        copy.start()
    rows_first.wait()
    tile(0, first_rows, True)
    wait_weights(n_copies)

    def later(index, carry):
        start = pl.multiple_of(first_rows + index * later_rows, LANES)
        tile(start, later_rows, False)
        return carry

    lax.fori_loop(0, (n_rows - first_rows) // later_rows, later, 0)


def encode(hidden_in, weights, first_rows, later_rows, chunk):
    rows = hidden_in.shape[0]
    up_weight, up_bias, down_weight, down_bias, norm_gain, norm_shift, proj_weight = weights
    width, hidden = up_weight.shape
    out_width = proj_weight.shape[1]
    n_copies = 2 * (hidden // chunk + 1)
    return pl.pallas_call(
        functools.partial(encode_kernel, first_rows, later_rows, chunk),
        in_specs=[HBM, HBM, VMEM, HBM, VMEM, VMEM, VMEM, VMEM],
        out_specs=VMEM,
        out_shape=jax.ShapeDtypeStruct((rows, out_width), jnp.bfloat16),
        scratch_shapes=[
            pltpu.VMEM((rows, width), jnp.bfloat16),
            pltpu.VMEM((width, hidden), jnp.bfloat16),
            pltpu.VMEM((hidden, width), jnp.bfloat16),
            pltpu.SemaphoreType.DMA((n_copies + 2,)),
        ],
        compiler_params=pltpu.CompilerParams(vmem_limit_bytes=ENC_BYTES),
        cost_estimate=pl.CostEstimate(
            flops=2 * rows * (2 * width * hidden + width * out_width),
            bytes_accessed=4 * width * hidden + 2 * rows * width,
            transcendentals=0,
        ),
        name="encode",
    )(hidden_in, up_weight, up_bias, down_weight, down_bias, norm_gain, norm_shift, proj_weight)


def body(
    hidden_in, up_weight, up_bias, down_weight, down_bias, norm_gain, norm_shift, proj_weight,
    centroids, lengths, owners, local_ids,
):
    n_devices = lax.axis_size("dp")
    token_rows = hidden_in.shape[0]
    width_out = proj_weight.shape[1]
    capacity = max(2, 2 * token_rows // n_devices)
    weights = (
        up_weight, up_bias, down_weight, down_bias, norm_gain, norm_shift, proj_weight,
    )
    slots, asked = plan(
        lengths, owners.reshape(-1, LANES), local_ids.reshape(-1, LANES), n_devices, capacity
    )
    arrived = lax.all_to_all(asked, "dp", split_axis=0, concat_axis=0, tiled=True)
    rows = gather_rows(arrived, centroids)
    hidden_in, rows = lax.optimization_barrier((hidden_in, rows))
    centers = lax.all_to_all(
        rows.reshape(n_devices, capacity, width_out), "dp", split_axis=0, concat_axis=0, tiled=True
    )
    embedded = encode(hidden_in, weights, 256, 768, 768)
    centers, embedded = lax.optimization_barrier((centers, embedded))
    return finish(slots, embedded, centers.reshape(-1, width_out))


def solution(mesh):
    in_specs = (
        P(("groups", "dp"), None),
        P(),
        P(),
        P(),
        P(),
        P(),
        P(),
        P(),
        P("dp", None),
        P(("groups", "dp")),
        P(("groups", "dp"), None),
        P(("groups", "dp")),
    )
    out_specs = P(("groups", "dp"), None)
    return jax.shard_map(body, mesh=mesh, in_specs=in_specs, out_specs=out_specs, check_vma=False)
```

```python
import functools

import jax
import jax.numpy as jnp
from jax import lax
from jax.experimental import pallas as pl
from jax.experimental.pallas import tpu as pltpu
from jax.sharding import PartitionSpec as P

LEN = 128
LANES = 128
LOW_BITS = 6
LOW = 1 << LOW_BITS
COUNT_SHIFT = 16
BLOCK = 32
VMEM_BYTES = 16 * 2**20
ENC_BYTES = 53 * 2**20
AHEAD = 10
FIRST_CHUNK = 256
VMEM = pl.BlockSpec(memory_space=pltpu.VMEM)
SMEM = pl.BlockSpec(memory_space=pltpu.SMEM)
HBM = pl.BlockSpec(memory_space=pltpu.HBM)
ANY = pl.BlockSpec(memory_space=pl.ANY)


def plan_kernel(lengths_ref, owners_ref, ids_ref, slots_ref, asked_ref):
    n_owners, capacity = asked_ref.shape
    n_rows = owners_ref.shape[0]
    owner_iota = lax.broadcasted_iota(jnp.int32, (n_owners, LANES), 0)
    slot_iota = lax.broadcasted_iota(jnp.int32, (capacity, LANES), 0)
    lane = lax.broadcasted_iota(jnp.int32, (1, LANES), 1)
    before = lax.broadcasted_iota(jnp.int32, (LANES, LANES), 0) < lax.broadcasted_iota(
        jnp.int32, (LANES, LANES), 1
    )
    counter = jnp.concatenate(
        [before.astype(jnp.float32), jnp.ones((LANES, LANES), jnp.float32)], axis=1
    ).astype(jnp.bfloat16)
    owner_rows = [owners_ref[row : row + 1, :] for row in range(n_rows)]
    live = [lane < lengths_ref[row] for row in range(n_rows)]
    hot = [
        ((owner_iota == owner_rows[row]) & live[row]).astype(jnp.float32) for row in range(n_rows)
    ]
    counts = jnp.dot(
        jnp.concatenate(hot, axis=0).astype(jnp.bfloat16),
        counter,
        preferred_element_type=jnp.float32,
    )
    named = jnp.zeros((n_owners, LANES), jnp.float32)
    placed, parts = [], []
    for row in range(n_rows):
        mine = counts[row * n_owners : (row + 1) * n_owners]
        slot = jnp.sum(hot[row] * (mine[:, :LANES] + named), axis=0, keepdims=True).astype(
            jnp.int32
        )
        named = named + mine[:, LANES:]
        slots_ref[n_rows + row : n_rows + row + 1, :] = jnp.full(
            (1, LANES), lengths_ref[row], jnp.int32
        )
        slots_ref[row : row + 1, :] = jnp.where(live[row], owner_rows[row] * capacity + slot, 0)
        placed.append((slot_iota == slot).astype(jnp.float32).astype(jnp.bfloat16))
        ids_row = ids_ref[row : row + 1, :]
        parts.append(
            jnp.concatenate(
                [
                    hot[row] * ((ids_row >> LOW_BITS)).astype(jnp.float32),
                    hot[row] * ((ids_row & (LOW - 1))).astype(jnp.float32),
                ],
                axis=0,
            ).astype(jnp.bfloat16)
        )
    both = lax.dot_general(
        jnp.concatenate(parts, axis=1),
        jnp.concatenate(placed, axis=1),
        (((1,), (1,)), ((), ())),
        preferred_element_type=jnp.float32,
    )
    ids = both[:n_owners].astype(jnp.int32) * LOW + both[n_owners:].astype(jnp.int32)
    first = lax.broadcasted_iota(jnp.int32, (n_owners, capacity), 1) == 0
    asked_ref[...] = ids + jnp.where(first, named[:, :capacity].astype(jnp.int32) << COUNT_SHIFT, 0)


def plan(lengths, owners, local_ids, n_owners, capacity):
    rows = owners.shape[0]
    return pl.pallas_call(
        plan_kernel,
        in_specs=[SMEM, VMEM, VMEM],
        out_specs=[VMEM, VMEM],
        out_shape=[
            jax.ShapeDtypeStruct((2 * rows, LANES), jnp.int32),
            jax.ShapeDtypeStruct((n_owners, capacity), jnp.int32),
        ],
        cost_estimate=pl.CostEstimate(flops=2 * 10**10, bytes_accessed=2**20, transcendentals=0),
        name="plan",
    )(lengths, owners, local_ids)


def gather_kernel(asked_hbm, table_ref, out_ref, asked_ref, table_f32, out_f32, arrived):
    n_owners, capacity = asked_ref.shape
    asked_copy = pltpu.make_async_copy(asked_hbm, asked_ref, arrived)
    asked_copy.start()
    table_f32[...] = table_ref[...].astype(jnp.float32)

    block = min(BLOCK, capacity)

    def device(source, carry):
        count = asked_ref[source, 0] >> COUNT_SHIFT
        base = source * capacity
        for start in range(0, capacity, block):

            @pl.when(count > start)
            def _():
                for slot in range(start, start + block):
                    row = asked_ref[source, slot]
                    if slot == 0:
                        row = row & ((1 << COUNT_SHIFT) - 1)
                    out_f32[pl.ds(base + slot, 1), :] = table_f32[pl.ds(row, 1), :]

        return carry

    asked_copy.wait()
    lax.fori_loop(0, n_owners, device, 0)
    out_ref[...] = out_f32[...].astype(jnp.bfloat16)


def gather_rows(asked, table):
    rows = asked.shape[0] * asked.shape[1]
    width = table.shape[1]
    return pl.pallas_call(
        gather_kernel,
        in_specs=[ANY, VMEM],
        out_specs=VMEM,
        out_shape=jax.ShapeDtypeStruct((rows, width), jnp.bfloat16),
        scratch_shapes=[
            pltpu.SMEM(asked.shape, jnp.int32),
            pltpu.VMEM(table.shape, jnp.float32),
            pltpu.VMEM((rows, width), jnp.float32),
            pltpu.SemaphoreType.DMA,
        ],
        compiler_params=pltpu.CompilerParams(vmem_limit_bytes=VMEM_BYTES),
        cost_estimate=pl.CostEstimate(flops=2 * 10**10, bytes_accessed=2**20, transcendentals=0),
        name="gather_rows",
    )(asked, table)


def finish_kernel(
    slots_hbm, embedded_ref, centers_ref, out_ref, slots_ref, centers_f32, mine, arrived
):
    slots_copy = pltpu.make_async_copy(slots_hbm, slots_ref, arrived)
    slots_copy.start()
    centers_f32[...] = centers_ref[...].astype(jnp.float32)
    n_passages = out_ref.shape[0] // LEN

    def passage_rows(passage, carry):
        length = slots_ref[n_passages + passage, 0]
        base = passage * LEN
        for start in range(0, LEN, BLOCK):

            @pl.when(length > start)
            def _():
                for position in range(start, start + BLOCK):
                    row = slots_ref[passage, position]
                    mine[pl.ds(base + position, 1), :] = centers_f32[pl.ds(row, 1), :]

        return carry

    slots_copy.wait()
    lax.fori_loop(0, n_passages, passage_rows, 0)
    position = lax.broadcasted_iota(jnp.int32, (LEN, 1), 0)
    for passage in range(n_passages):
        at = slice(passage * LEN, (passage + 1) * LEN)
        difference = embedded_ref[at, :].astype(jnp.float32) - mine[at, :]
        total = jnp.sum(difference * difference, axis=1, keepdims=True)
        result = difference * lax.rsqrt(total + 1e-06)
        alive = position < slots_ref[n_passages + passage, 0]
        out_ref[at, :] = jnp.where(alive, result, 0.0).astype(jnp.bfloat16)


def finish(slots, embedded, centers):
    rows = embedded.shape[0]
    width = centers.shape[1]
    return pl.pallas_call(
        finish_kernel,
        in_specs=[ANY, VMEM, VMEM],
        out_specs=VMEM,
        out_shape=jax.ShapeDtypeStruct((rows, width), jnp.bfloat16),
        scratch_shapes=[
            pltpu.SMEM(slots.shape, jnp.int32),
            pltpu.VMEM(centers.shape, jnp.float32),
            pltpu.VMEM((rows, width), jnp.float32),
            pltpu.SemaphoreType.DMA,
        ],
        compiler_params=pltpu.CompilerParams(vmem_limit_bytes=VMEM_BYTES),
        name="finish",
    )(slots, embedded, centers)


def encode_kernel(
    first_rows, later_rows, chunk, rows_hbm, up_hbm, up_bias, down_hbm, down_bias, gain, shift, proj, out_ref,
    rows_vmem, up_vmem, down_vmem, arrived,
):
    hidden = up_vmem.shape[1]
    later_bounds = list(range(0, hidden + 1, chunk))
    first_bounds = [0, FIRST_CHUNK] + later_bounds[1:]
    n_copies = 2 * (len(first_bounds) - 1)
    queue = []
    for low, high in zip(first_bounds, first_bounds[1:]):
        at = pl.ds(low, high - low)
        semaphores = [arrived.at[len(queue)], arrived.at[len(queue) + 1]]
        queue += [
            pltpu.make_async_copy(up_hbm.at[:, at], up_vmem.at[:, at], semaphores[0]),
            pltpu.make_async_copy(down_hbm.at[at, :], down_vmem.at[at, :], semaphores[1]),
        ]

    def rows_copy(start, count, semaphore):
        at = pl.ds(start, count)
        return pltpu.make_async_copy(rows_hbm.at[at, :], rows_vmem.at[at, :], semaphore)

    n_rows = out_ref.shape[0]
    rows_first = rows_copy(0, first_rows, arrived.at[n_copies])
    queue.append(rows_copy(first_rows, n_rows - first_rows, arrived.at[n_copies + 1]))

    def wait_weights(index):
        queue[index].wait()
        for copy in queue[index + AHEAD : index + AHEAD + 1]:
            copy.start()

    def tile(start, count, first):
        at = pl.ds(start, count)
        rows = rows_vmem[at, :]

        bounds = first_bounds if first else later_bounds
        n_chunks = len(bounds) - 1

        def up(index):
            part = slice(bounds[index], bounds[index + 1])
            return (
                jnp.dot(rows, up_vmem[:, part], preferred_element_type=jnp.float32)
                + up_bias[part][None, :]
            )

        total = None
        if first:
            wait_weights(0)
        up_proj = up(0)
        for index in range(n_chunks):
            if first:
                wait_weights(2 * index + 1)
                if index + 1 < n_chunks:
                    wait_weights(2 * index + 2)
            following = up(index + 1) if index + 1 < n_chunks else None
            activated = (0.5 * up_proj * (1.0 + lax.erf(up_proj * 0.7071067811865476))).astype(
                jnp.bfloat16
            )
            part = jnp.dot(
                activated,
                down_vmem[bounds[index] : bounds[index + 1], :],
                preferred_element_type=jnp.float32,
            )
            total = part if total is None else total + part
            up_proj = following
        ffn_out = total + down_bias[...][None, :] + rows.astype(jnp.float32)
        center = jnp.mean(ffn_out, axis=1, keepdims=True)
        centered = ffn_out - center
        spread = jnp.mean(centered * centered, axis=1, keepdims=True)
        normed = (
            centered * lax.rsqrt(spread + 1e-05) * gain[...][None, :] + shift[...][None, :]
        ).astype(jnp.bfloat16)
        projected = jnp.dot(normed, proj[...], preferred_element_type=jnp.float32)
        size = jnp.sum(projected * projected, axis=1, keepdims=True)
        out_ref[at, :] = (projected * lax.rsqrt(size + 1e-06)).astype(jnp.bfloat16)

    rows_first.start()
    for copy in queue[:AHEAD]:
        copy.start()
    rows_first.wait()
    tile(0, first_rows, True)
    wait_weights(n_copies)

    def later(index, carry):
        start = pl.multiple_of(first_rows + index * later_rows, LANES)
        tile(start, later_rows, False)
        return carry

    lax.fori_loop(0, (n_rows - first_rows) // later_rows, later, 0)


def encode(hidden_in, weights, first_rows, later_rows, chunk):
    rows = hidden_in.shape[0]
    up_weight, up_bias, down_weight, down_bias, norm_gain, norm_shift, proj_weight = weights
    width, hidden = up_weight.shape
    out_width = proj_weight.shape[1]
    n_copies = 2 * (hidden // chunk + 1)
    return pl.pallas_call(
        functools.partial(encode_kernel, first_rows, later_rows, chunk),
        in_specs=[HBM, HBM, VMEM, HBM, VMEM, VMEM, VMEM, VMEM],
        out_specs=VMEM,
        out_shape=jax.ShapeDtypeStruct((rows, out_width), jnp.bfloat16),
        scratch_shapes=[
            pltpu.VMEM((rows, width), jnp.bfloat16),
            pltpu.VMEM((width, hidden), jnp.bfloat16),
            pltpu.VMEM((hidden, width), jnp.bfloat16),
            pltpu.SemaphoreType.DMA((n_copies + 2,)),
        ],
        compiler_params=pltpu.CompilerParams(vmem_limit_bytes=ENC_BYTES),
        cost_estimate=pl.CostEstimate(
            flops=2 * rows * (2 * width * hidden + width * out_width),
            bytes_accessed=4 * width * hidden + 2 * rows * width,
            transcendentals=0,
        ),
        name="encode",
    )(hidden_in, up_weight, up_bias, down_weight, down_bias, norm_gain, norm_shift, proj_weight)


def body(
    hidden_in, up_weight, up_bias, down_weight, down_bias, norm_gain, norm_shift, proj_weight,
    centroids, lengths, owners, local_ids,
):
    n_devices = lax.axis_size("dp")
    token_rows = hidden_in.shape[0]
    width_out = proj_weight.shape[1]
    capacity = max(2, 2 * token_rows // n_devices)
    weights = (
        up_weight, up_bias, down_weight, down_bias, norm_gain, norm_shift, proj_weight,
    )
    slots, asked = plan(
        lengths, owners.reshape(-1, LANES), local_ids.reshape(-1, LANES), n_devices, capacity
    )
    arrived = lax.all_to_all(asked, "dp", split_axis=0, concat_axis=0, tiled=True)
    rows = gather_rows(arrived, centroids)
    hidden_in, rows = lax.optimization_barrier((hidden_in, rows))
    centers = lax.all_to_all(
        rows.reshape(n_devices, capacity, width_out), "dp", split_axis=0, concat_axis=0, tiled=True
    )
    embedded = encode(hidden_in, weights, 256, 768, 768)
    centers, embedded = lax.optimization_barrier((centers, embedded))
    return finish(slots, embedded, centers.reshape(-1, width_out))


def solution(mesh):
    in_specs = (
        P(("groups", "dp"), None),
        P(),
        P(),
        P(),
        P(),
        P(),
        P(),
        P(),
        P("dp", None),
        P(("groups", "dp")),
        P(("groups", "dp"), None),
        P(("groups", "dp")),
    )
    out_specs = P(("groups", "dp"), None)
    return jax.shard_map(body, mesh=mesh, in_specs=in_specs, out_specs=out_specs, check_vma=False)
```
